1024 devices in a mesh: dp: 16 (over x, y), fsdp: 64 (over z, core).
Axes of the slice: x: 4, y: 4, z: 32, core: 2. Of those that a mesh axis runs over, the one named last changes fastest.
Arguments:
- grad: bfloat16 [64, 16, 4, 16384], P('fsdp', 'dp'), may hold values from -19 to 19
- block_owner: int32 [256], replicated, may hold values from 0 to 63, as said below
- left: float32 [64, 4, 8, 16, 4, 512], P('fsdp', None, None, 'dp'), may hold values from -6 to 6
- right: float32 [64, 4, 8, 16, 4, 512], P('fsdp', None, None, 'dp'), may hold values from -6 to 6
- left_root: bfloat16 [64, 4, 8, 16, 4, 512], P('fsdp', None, None, 'dp'), may hold values from -0.125 to 4.625
- right_root: bfloat16 [64, 4, 8, 16, 4, 512], P('fsdp', None, None, 'dp'), may hold values from -0.125 to 1.625
- moment: float32 [64, 4, 8, 16, 4, 512], P('fsdp', None, None, 'dp'), may hold values from 0.05 to 2
Outputs:
- update: bfloat16 [64, 16, 4, 16384], P('fsdp', 'dp')
- left_new: float32 [64, 4, 8, 16, 4, 512], P('fsdp', None, None, 'dp')
- right_new: float32 [64, 4, 8, 16, 4, 512], P('fsdp', None, None, 'dp')
- moment_new: float32 [64, 4, 8, 16, 4, 512], P('fsdp', None, None, 'dp')
The draws below stay inside these ranges and needn't reach their ends.
Inputs may be any that keep to these rules, and one draw needn't show every extreme that they name: `block_owner`: each of the 64 owners holds exactly 4 blocks and at most 1 block of one band; every owner of a band holds exactly 1 of its blocks.
All inputs are finite; a program needn't handle non-finite values.
Results may differ from the reference program's by a relative error of at most 0.0049.
Values may be sent and summed in bfloat16 or wider, within the bound.
No kernel may reach another device: no remote copies, remote signals or barrier semaphores. Data moves between devices by JAX's collectives and lax.ppermute only.
A program may use at most 128 MiB of HBM per device.

```python
import math
import jax
import jax.numpy as jnp
from jax import lax

B = 512
COLS = 16384
R_F = 64
ROWS = 4096
ROW_DEV = 4
SPB = 8
NBAND = 8
CB = 32
NB = 256
K = 4
OWNERS_BAND = 32
CAP = 1
N_DP = 16
N_FSDP = 64


def draw_grad(key, part):
    key = jax.random.fold_in(key, 5)
    grid_shape = (N_FSDP, N_DP, ROW_DEV, COLS)
    value_key = jax.random.fold_in(key, 1)
    weight_key = jax.random.fold_in(key, 4)
    common_key = jax.random.fold_in(key, 6)
    base_value = 0.8 * jax.random.truncated_normal(value_key, -6.0, 6.0, grid_shape)
    row_weight = jax.random.uniform(weight_key, (N_FSDP, N_DP, ROW_DEV, 1), minval=0.2, maxval=0.5)
    common_part = jax.random.truncated_normal(common_key, -4.0, 4.0, (1, 1, 1, COLS))
    result_value = base_value + row_weight * common_part
    return result_value.astype(jnp.bfloat16)


def draw_block_owner(key, part):
    key = jax.random.fold_in(key, 11)
    owner_order = jax.random.permutation(jax.random.fold_in(key, 1), N_FSDP)
    band_keys = jax.random.split(jax.random.fold_in(key, 2), NBAND)
    col_order = jax.vmap(lambda band_key: jax.random.permutation(band_key, CB))(band_keys)
    col_rank = jnp.argsort(col_order, axis=1)
    band_start = jnp.arange(NBAND, dtype=jnp.int32)[:, None] * OWNERS_BAND
    owner_pos = (band_start + col_rank // CAP) % N_FSDP
    return owner_order[owner_pos].reshape(NB).astype(jnp.int32)


def root_matrix(key, slope, top_value, offset):
    diagonal = jax.random.uniform(jax.random.fold_in(key, 1), (N_FSDP, K, B), minval=0.5, maxval=1.5)
    row_index = jnp.arange(B, dtype=jnp.int32)
    replica = row_index % R_F // ROW_DEV
    rising = 1.0 + slope * replica.astype(jnp.float32) / (N_DP - 1)
    identity = jnp.eye(B, dtype=jnp.float32)
    spread = 0.03 * jax.random.truncated_normal(jax.random.fold_in(key, 2), -4.0, 4.0, (N_FSDP, K, B, B)) + offset * (1.0 - identity)
    matrix = identity * (diagonal * rising)[..., None] + spread
    top_row = (N_DP - 1) * ROW_DEV
    matrix = matrix.at[0, 0, top_row, top_row].set(top_value)
    matrix = matrix.at[0, 0, 0, 1].set(-0.125)
    return matrix.reshape(N_FSDP, K, SPB, N_DP, ROW_DEV, B).astype(jnp.bfloat16)


def draw_left_root(key, part):
    key = jax.random.fold_in(key, 7)
    offset = 0.005
    return root_matrix(key, 2.0, 4.625, offset)


def draw_right_root(key, part):
    key = jax.random.fold_in(key, 9)
    return root_matrix(key, 0.0, 1.625, 0.0)


def steps_of(own_key, extent, cuts, low, high):
    def one(position, shards_of):
        draws = jax.random.uniform(jax.random.fold_in(jax.random.fold_in(own_key, 6), position), (shards_of,), jnp.float32, low / len(cuts), high / len(cuts))
        return jnp.repeat(jnp.exp(draws), extent[position] // shards_of).reshape((-1,) + (1,) * (len(extent) - position - 1))

    factor_of = one(*cuts[0])
    for cut in cuts[1:]:
        factor_of = factor_of * one(*cut)
    return factor_of


def normal_values(stream_key, extent, scale, reach, cuts=(), kind=jnp.bfloat16):
    values = jax.random.normal(stream_key, extent, jnp.float32) * scale
    if len(cuts) > 0:
        values = steps_of(stream_key, extent, cuts, -0.22, 0.18) * values
    return jnp.clip(values, min=-reach, max=reach).astype(kind)


def setup_inputs(seed: int = 0) -> dict:
    streams_of = jax.random.split(jax.random.key(seed), 8)
    return {
        "grad": draw_grad(jax.random.fold_in(streams_of[7], 71), 0),
        "block_owner": draw_block_owner(jax.random.fold_in(streams_of[7], 71), 0),
        "left": normal_values(streams_of[2], (N_FSDP, K, SPB, N_DP, ROW_DEV, B), 1.0, 6.0, ((0, 64), (3, 16)), jnp.float32),
        "right": normal_values(streams_of[3], (N_FSDP, K, SPB, N_DP, ROW_DEV, B), 1.0, 6.0, ((0, 64), (3, 16)), jnp.float32),
        "left_root": draw_left_root(jax.random.fold_in(streams_of[7], 71), 0),
        "right_root": draw_right_root(jax.random.fold_in(streams_of[7], 71), 0),
        "moment": jnp.clip(jnp.exp(math.log(2.0) - 3.6888794 * jax.random.uniform(streams_of[6], (N_FSDP, K, SPB, N_DP, ROW_DEV, B), jnp.float32) ** steps_of(streams_of[6], (N_FSDP, K, SPB, N_DP, ROW_DEV, B), ((0, 64), (3, 16)), -0.2, 0.2)), 0.05, 2.0),
    }


FACTOR_DECAY = 0.999
MOMENT_DECAY = 0.95
ADAM_EPS = 1e-08
NORM_EPS = 1e-06

def slot_order(block_owner):
    block_ids = jnp.arange(NB, dtype=jnp.int32)
    earlier = block_ids[None, :] < block_ids[:, None]
    same_owner = block_owner[None, :] == block_owner[:, None]
    slot_rank = lax.optimization_barrier(jnp.sum(jnp.logical_and(same_owner, earlier).astype(jnp.int32), axis=1))
    slot_table = jnp.zeros((N_FSDP, K), jnp.int32).at[block_owner, slot_rank].set(block_ids)
    return slot_table.reshape(N_FSDP * K)

def reference(grad, block_owner, left, right, left_root, right_root, moment):
    full_grad = grad.reshape(ROWS, COLS)
    slot_table = slot_order(block_owner)
    slot_shape = (N_FSDP * K, B, B)

    def per_block(operands):
        block_index, left_block, right_block, left_inv, right_inv, moment_block = operands
        band_index = (block_index // CB).astype(jnp.int32)
        column = (block_index % CB).astype(jnp.int32)
        grad_block = lax.dynamic_slice(full_grad, (band_index * B, column * B), (B, B))
        left_out = FACTOR_DECAY * left_block + (1.0 - FACTOR_DECAY) * jnp.dot(grad_block, grad_block.T, preferred_element_type=jnp.float32)
        right_out = FACTOR_DECAY * right_block + (1.0 - FACTOR_DECAY) * jnp.dot(grad_block.T, grad_block, preferred_element_type=jnp.float32)
        values = grad_block.astype(jnp.float32)
        moment_out = MOMENT_DECAY * moment_block + (1.0 - MOMENT_DECAY) * values * values
        adam_step = values / (jnp.sqrt(moment_out) + ADAM_EPS)
        left_mixed = jnp.dot(left_inv, grad_block, preferred_element_type=jnp.float32).astype(jnp.bfloat16)
        precond = jnp.dot(left_mixed, right_inv, preferred_element_type=jnp.float32)
        graft_scale = jnp.sqrt(jnp.sum(adam_step * adam_step)) / jnp.sqrt(jnp.sum(precond * precond) + NORM_EPS)
        return (left_out, right_out, moment_out, (precond * graft_scale).astype(jnp.bfloat16))
    left_new, right_new, moment_new, blocks_out = lax.map(per_block, (slot_table, left.reshape(slot_shape), right.reshape(slot_shape), left_root.reshape(slot_shape), right_root.reshape(slot_shape), moment.reshape(slot_shape)))
    placed = jnp.zeros((NB, B, B), jnp.bfloat16).at[slot_table].set(blocks_out)
    update = placed.reshape(NBAND, CB, B, B).transpose(0, 2, 1, 3).reshape(N_FSDP, N_DP, ROW_DEV, COLS)
    return (update, left_new.reshape(left.shape), right_new.reshape(right.shape), moment_new.reshape(moment.shape))
```

```python
import functools
import jax
import jax.numpy as jnp
from jax import lax
from jax.experimental import pallas as pl
from jax.experimental.pallas import tpu as pltpu
from jax.sharding import PartitionSpec as P

FACTOR_DECAY = 0.999
MOMENT_DECAY = 0.95
ADAM_EPS = 1e-08
NORM_EPS = 1e-06
VMEM_LIMIT = 32 * 1024 * 1024
NORM_ROWS = 8

SMEM = pl.BlockSpec(memory_space=pltpu.SMEM)
VMEM = pl.BlockSpec(memory_space=pltpu.VMEM)


def call(kernel, out_shape, in_specs, out_specs, scratch_shapes=()):
    return pl.pallas_call(
        kernel,
        out_shape=out_shape,
        in_specs=in_specs,
        out_specs=out_specs,
        scratch_shapes=scratch_shapes,
        compiler_params=pltpu.CompilerParams(vmem_limit_bytes=VMEM_LIMIT),
    )


def dot(a, b, contract=(1, 0)):
    return lax.dot_general(
        a, b, (((contract[0],), (contract[1],)), ((), ())), preferred_element_type=jnp.float32
    )


def send_rows_kernel(shards, owner_ref, grad_ref, out_ref):
    width = out_ref.shape[2]
    count = grad_ref.shape[1] // width
    band = lax.axis_index("fsdp") // shards
    for column in range(count):
        owner = owner_ref[band * count + column]
        out_ref[owner] = grad_ref[:, column * width : (column + 1) * width]


def own_rows_kernel(
    band_ref, arrived_ref, moment_ref, left_ref, right_ref, out_ref, moment_out_ref, rows_ref
):
    slots, shards, dev_rows, width = moment_ref.shape
    rows = shards * dev_rows
    copies = out_ref.shape[0] // slots
    for slot in range(slots):
        band = band_ref[slot]
        total = jnp.zeros((dev_rows, width), jnp.float32)
        for shard in range(shards):
            values = arrived_ref[band * shards + shard].astype(jnp.float32)
            moment = (
                MOMENT_DECAY * moment_ref[slot, shard] + (1.0 - MOMENT_DECAY) * values * values
            )
            moment_out_ref[slot, shard] = moment
            adam = values / (jnp.sqrt(moment) + ADAM_EPS)
            total += adam * adam
            rows_ref[shard * dev_rows : (shard + 1) * dev_rows, :] = values
        own = rows_ref[...].astype(jnp.bfloat16)
        whole = jnp.sum(total, axis=(0, 1), keepdims=True)
        high = whole.astype(jnp.bfloat16).astype(jnp.float32)
        lane = lax.broadcasted_iota(jnp.int32, (NORM_ROWS, width), 1)
        norm = jnp.where(lane < width // 2, high, whole - high).astype(jnp.bfloat16)
        for copy in range(copies):
            place = copy * slots + slot
            out_ref[place, :rows, :] = own
            out_ref[place, rows : 2 * rows, :] = left_ref[slot]
            out_ref[place, 2 * rows : 3 * rows, :] = right_ref[slot]
            out_ref[place, 3 * rows :, :] = norm


def block_kernel(rows, slots, arrived_ref, order_ref, out_ref, grad_ref, precond_ref):
    width = order_ref.shape[0]
    span = slots * rows
    first = pl.multiple_of(lax.axis_index("dp") // slots * span, span)
    order = order_ref[...]
    grad = arrived_ref[:, :rows, :].reshape(width, width)
    left_root = arrived_ref[:, rows : 2 * rows, :].reshape(width, width)
    right_root = arrived_ref[:, 2 * rows : 3 * rows, :].reshape(width, width)
    by_device = dot(grad, order).astype(jnp.bfloat16)
    grad_ref[...] = by_device
    mixed = dot(left_root, by_device).astype(jnp.bfloat16)
    precond = dot(mixed, right_root)
    precond_ref[...] = precond
    norms = jnp.sum(arrived_ref[:, 3 * rows :, :].astype(jnp.float32), axis=0)
    half = width // 2
    adam_total = norms[:1, :1] + norms[:1, half : half + 1]
    precond_total = jnp.sum(precond * precond, axis=(0, 1), keepdims=True)
    scale = jnp.sqrt(adam_total) / jnp.sqrt(precond_total + NORM_EPS)
    update = (precond_ref[pl.ds(first, span), :] * scale).astype(jnp.bfloat16)
    left_gram = dot(grad_ref[pl.ds(first, span), :], by_device, (1, 1)).astype(jnp.bfloat16)
    left_gram = dot(left_gram, order, (1, 1)).astype(jnp.bfloat16)
    right_gram = dot(grad_ref[:, pl.ds(first, span)], grad, (0, 0)).astype(jnp.bfloat16)
    for place in range(slots):
        part = slice(place * rows, (place + 1) * rows)
        out_ref[place, :rows, :] = update[part]
        out_ref[place, rows : 2 * rows, :] = left_gram[part]
        out_ref[place, 2 * rows :, :] = right_gram[part]


def return_rows_kernel(shards, dev_rows, band_ref, back_ref, out_ref):
    for slot in range(back_ref.shape[0]):
        band = band_ref[slot]
        for shard in range(shards):
            out_ref[band * shards + shard] = back_ref[
                slot, shard * dev_rows : (shard + 1) * dev_rows, :
            ]


def place_rows_kernel(shards, owner_ref, returned_ref, out_ref):
    width = returned_ref.shape[2]
    count = out_ref.shape[1] // width
    band = lax.axis_index("fsdp") // shards
    for column in range(count):
        owner = owner_ref[band * count + column]
        out_ref[:, column * width : (column + 1) * width] = returned_ref[owner]


def owned_bands(block_owner, owner, slots, columns):
    ids = jnp.arange(block_owner.shape[0], dtype=jnp.int32)
    mine = block_owner == owner
    rank = jnp.sum((mine[None, :] & (ids[None, :] < ids[:, None])).astype(jnp.int32), axis=1)
    slot = jnp.arange(slots, dtype=jnp.int32)
    held = mine[None, :] & (rank[None, :] == slot[:, None])
    return jnp.sum(jnp.where(held, ids[None, :] // columns, 0), axis=1)


def device_order(shards, replicas, dev_rows):
    width = shards * replicas * dev_rows
    place = jnp.arange(width, dtype=jnp.int32)
    device, rest = place // (shards * dev_rows), place % (shards * dev_rows)
    row = (rest // dev_rows * replicas + device) * dev_rows + rest % dev_rows
    return (place[:, None] == row[None, :]).astype(jnp.bfloat16)


def body(grad, block_owner, left, right, left_root, right_root, moment):
    replicas = lax.axis_size("dp")
    owners = lax.axis_size("fsdp")
    dev_rows, columns_all = grad.shape[2:]
    _, slots, shards, _, _, width = left.shape
    rows = shards * dev_rows
    columns = columns_all // width
    groups = [list(range(i, i + slots)) for i in range(0, replicas, slots)]
    pieces = (owners, dev_rows, width)
    by_piece = (slots, shards, dev_rows, width)

    outgoing = call(
        functools.partial(send_rows_kernel, shards),
        jax.ShapeDtypeStruct(pieces, jnp.bfloat16),
        [SMEM, VMEM],
        VMEM,
    )(block_owner, grad.reshape(dev_rows, columns_all))
    arrived = lax.all_to_all(outgoing, "fsdp", split_axis=0, concat_axis=0, tiled=True)

    bands = owned_bands(block_owner, lax.axis_index("fsdp"), slots, columns)
    order = device_order(shards, replicas, dev_rows)
    left_rows = dot(left_root.reshape(slots * rows, width), order).astype(jnp.bfloat16)
    packed, moment_new = call(
        own_rows_kernel,
        (
            jax.ShapeDtypeStruct((replicas, 3 * rows + NORM_ROWS, width), jnp.bfloat16),
            jax.ShapeDtypeStruct(by_piece, jnp.float32),
        ),
        [SMEM, VMEM, VMEM, VMEM, VMEM],
        (VMEM, VMEM),
        [pltpu.VMEM((rows, width), jnp.float32)],
    )(
        bands,
        arrived,
        moment.reshape(by_piece),
        left_rows.reshape(slots, rows, width),
        right_root.reshape(slots, rows, width),
    )
    gathered = lax.all_to_all(packed, "dp", split_axis=0, concat_axis=0, tiled=True)

    results = call(
        functools.partial(block_kernel, rows, slots),
        jax.ShapeDtypeStruct((slots, 3 * rows, width), jnp.bfloat16),
        [VMEM, VMEM],
        VMEM,
        [pltpu.VMEM((width, width), jnp.bfloat16), pltpu.VMEM((width, width), jnp.float32)],
    )(gathered, order)
    back = lax.all_to_all(
        results, "dp", split_axis=0, concat_axis=0, tiled=True, axis_index_groups=groups
    )

    returning = call(
        functools.partial(return_rows_kernel, shards, dev_rows),
        jax.ShapeDtypeStruct(pieces, jnp.bfloat16),
        [SMEM, VMEM],
        VMEM,
    )(bands, back)
    returned = lax.all_to_all(returning, "fsdp", split_axis=0, concat_axis=0, tiled=True)
    update = call(
        functools.partial(place_rows_kernel, shards),
        jax.ShapeDtypeStruct((dev_rows, columns_all), jnp.bfloat16),
        [SMEM, VMEM],
        VMEM,
    )(block_owner, returned)

    def factor(old, gram):
        gram = gram.astype(jnp.float32).reshape(old.shape)
        return FACTOR_DECAY * old + (1.0 - FACTOR_DECAY) * gram

    return (
        update.reshape(grad.shape),
        factor(left, back[:, rows : 2 * rows]),
        factor(right, back[:, 2 * rows :]),
        moment_new.reshape(moment.shape),
    )


def solution(mesh):
    state = P("fsdp", None, None, "dp", None, None)
    rows = P("fsdp", "dp", None, None)
    return jax.shard_map(
        body,
        mesh=mesh,
        in_specs=(rows, P(), state, state, state, state, state),
        out_specs=(rows, state, state, state),
        check_vma=False,
    )
```

```python
import functools
import jax
import jax.numpy as jnp
from jax import lax
from jax.experimental import pallas as pl
from jax.experimental.pallas import tpu as pltpu
from jax.sharding import PartitionSpec as P

FACTOR_DECAY = 0.999
MOMENT_DECAY = 0.95
ADAM_EPS = 1e-08
NORM_EPS = 1e-06
VMEM_LIMIT = 32 * 1024 * 1024
NORM_ROWS = 8

SMEM = pl.BlockSpec(memory_space=pltpu.SMEM)
VMEM = pl.BlockSpec(memory_space=pltpu.VMEM)
ANY = pl.BlockSpec(memory_space=pl.ANY)


ORDER_STEP = 31
ORDER_FIRST = 22


def place_of(owner, owners):
    half = owners // 2
    back = pow(ORDER_STEP, -1, half)
    return lax.rem(owner, 2) * half + lax.rem((owner // 2 + half - ORDER_FIRST) * back, half)


def exchange_order(owners):
    half = owners // 2
    chips = [(ORDER_FIRST + i * ORDER_STEP) % half for i in range(half)]
    return [[2 * chip + core for core in range(2) for chip in chips]]


def call(kernel, out_shape, in_specs, out_specs, scratch_shapes=()):
    return pl.pallas_call(
        kernel,
        out_shape=out_shape,
        in_specs=in_specs,
        out_specs=out_specs,
        scratch_shapes=scratch_shapes,
        compiler_params=pltpu.CompilerParams(vmem_limit_bytes=VMEM_LIMIT),
    )


def dot(a, b, contract=(1, 0)):
    return lax.dot_general(
        a, b, (((contract[0],), (contract[1],)), ((), ())), preferred_element_type=jnp.float32
    )


def send_rows_kernel(shards, owner_ref, grad_ref, out_ref):
    width = out_ref.shape[2]
    count = grad_ref.shape[1] // width
    band = lax.axis_index("fsdp") // shards
    for column in range(count):
        owner = owner_ref[band * count + column]
        out_ref[place_of(owner, out_ref.shape[0])] = grad_ref[:, column * width : (column + 1) * width]


def own_rows_kernel(band_ref, arrived_ref, moment_ref, *refs):
    out_ref, moment_out_ref, rows_ref = refs[-3:]
    slots, shards, dev_rows, width = moment_ref.shape
    owners = arrived_ref.shape[0]
    rows = shards * dev_rows
    copies = out_ref.shape[0] // slots
    for slot in range(slots):
        band = band_ref[slot]
        total = jnp.zeros((dev_rows, width), jnp.float32)
        for shard in range(shards):
            values = arrived_ref[place_of(band * shards + shard, owners)].astype(jnp.float32)
            moment = (
                MOMENT_DECAY * moment_ref[slot, shard] + (1.0 - MOMENT_DECAY) * values * values
            )
            moment_out_ref[slot, shard] = moment
            adam = values / (jnp.sqrt(moment) + ADAM_EPS)
            total += adam * adam
            rows_ref[shard * dev_rows : (shard + 1) * dev_rows, :] = values
        own = rows_ref[...].astype(jnp.bfloat16)
        whole = jnp.sum(total, axis=(0, 1), keepdims=True)
        high = whole.astype(jnp.bfloat16).astype(jnp.float32)
        lane = lax.broadcasted_iota(jnp.int32, (NORM_ROWS, width), 1)
        norm = jnp.where(lane < width // 2, high, whole - high).astype(jnp.bfloat16)
        for copy in range(copies):
            place = copy * slots + slot
            out_ref[place, :rows, :] = own
            out_ref[place, rows:, :] = norm


def split_roots_kernel(left_ref, right_ref, order_ref, *refs):
    out_refs, rows_ref = refs[:-1], refs[-1]
    slots, rows, width = right_ref.shape
    place = lax.rem(lax.axis_index("dp"), slots)
    left = dot(left_ref[...].reshape(slots * rows, width), order_ref[...])
    rows_ref[...] = left.astype(jnp.bfloat16).reshape(slots, rows, width)
    for step, out_ref in enumerate(out_refs):
        slot = lax.rem(place + step, slots)
        out_ref[:rows, :] = rows_ref[slot]
        out_ref[rows:, :] = right_ref[slot]


def block_kernel(rows, slots, arrived_ref, order_ref, *refs):
    *root_refs, out_ref, precond_ref, left_ref, right_ref = refs
    width = order_ref.shape[0]
    span = slots * rows
    device = lax.axis_index("dp")
    first = pl.multiple_of(device // slots * span, span)
    lines = len(root_refs)
    for step, root_ref in enumerate(root_refs):
        line = lax.rem(device // slots + lines - step, lines)
        for part in range(slots):
            source = line * slots + lax.rem(device + slots - part, slots)
            place = pl.ds(pl.multiple_of(source * rows, rows), rows)
            left_ref[place, :] = root_ref[2 * part * rows : (2 * part + 1) * rows, :]
            right_ref[place, :] = root_ref[(2 * part + 1) * rows : (2 * part + 2) * rows, :]
    order = order_ref[...]
    grad = arrived_ref[:, :rows, :].reshape(width, width)
    by_device = dot(grad, order).astype(jnp.bfloat16)
    mixed = dot(left_ref[...], by_device).astype(jnp.bfloat16)
    precond = dot(mixed, right_ref[...])
    precond_ref[...] = precond
    norms = jnp.sum(arrived_ref[:, rows:, :].astype(jnp.float32), axis=0)
    half = width // 2
    adam_total = norms[:1, :1] + norms[:1, half : half + 1]
    precond_total = jnp.sum(precond * precond, axis=(0, 1), keepdims=True)
    scale = jnp.sqrt(adam_total) / jnp.sqrt(precond_total + NORM_EPS)
    update = (precond_ref[pl.ds(first, span), :] * scale).astype(jnp.bfloat16)
    for place in range(slots):
        out_ref[place] = update[place * rows : (place + 1) * rows]


def gram_kernel(rows, arrived_ref, order_ref, _, *refs):
    out_refs, grad_ref = refs[:-1], refs[-1]
    slots = len(out_refs)
    width = order_ref.shape[0]
    device = lax.axis_index("dp")
    order = order_ref[...]
    grad = arrived_ref[:, :rows, :].reshape(width, width)
    by_device = dot(grad, order).astype(jnp.bfloat16)
    grad_ref[...] = by_device
    span = slots * rows
    first = pl.multiple_of(device // slots * span, span)
    left_gram = dot(grad_ref[pl.ds(first, span), :], by_device, (1, 1)).astype(jnp.bfloat16)
    left_gram = dot(left_gram, order, (1, 1)).astype(jnp.bfloat16)
    right_gram = dot(grad_ref[:, pl.ds(first, span)], grad, (0, 0)).astype(jnp.bfloat16)
    for step, out_ref in enumerate(out_refs):
        for place in range(slots):

            @pl.when(lax.rem(device + step, slots) == place)
            def _():
                part = slice(place * rows, (place + 1) * rows)
                out_ref[:rows, :] = left_gram[part]
                out_ref[rows:, :] = right_gram[part]


def return_rows_kernel(shards, dev_rows, band_ref, back_ref, out_ref):
    for slot in range(back_ref.shape[0]):
        band = band_ref[slot]
        for shard in range(shards):
            out_ref[place_of(band * shards + shard, out_ref.shape[0])] = back_ref[
                slot, shard * dev_rows : (shard + 1) * dev_rows, :
            ]


def place_rows_kernel(shards, owner_ref, returned_ref, out_ref):
    width = returned_ref.shape[2]
    count = out_ref.shape[1] // width
    band = lax.axis_index("fsdp") // shards
    for column in range(count):
        owner = owner_ref[band * count + column]
        out_ref[:, column * width : (column + 1) * width] = returned_ref[
            place_of(owner, returned_ref.shape[0])
        ]


def factors_kernel(left_ref, right_ref, *refs):
    gram_refs, out_refs = refs[:-2], refs[-2:]
    slots, shards, dev_rows, _ = left_ref.shape
    rows = shards * dev_rows
    place = lax.rem(lax.axis_index("dp"), slots)
    for step, gram_ref in enumerate(gram_refs):
        slot = lax.rem(place + slots - step, slots)
        for side, (old_ref, out_ref) in enumerate(zip((left_ref, right_ref), out_refs)):
            for shard in range(shards):
                first = side * rows + shard * dev_rows
                gram = gram_ref[first : first + dev_rows, :].astype(jnp.float32)
                out_ref[slot, shard] = (
                    FACTOR_DECAY * old_ref[slot, shard] + (1.0 - FACTOR_DECAY) * gram
                )


def owned_bands(block_owner, owner, slots, columns):
    ids = jnp.arange(block_owner.shape[0], dtype=jnp.int32)
    mine = block_owner == owner
    rank = jnp.sum((mine[None, :] & (ids[None, :] < ids[:, None])).astype(jnp.int32), axis=1)
    slot = jnp.arange(slots, dtype=jnp.int32)
    held = mine[None, :] & (rank[None, :] == slot[:, None])
    return jnp.sum(jnp.where(held, ids[None, :] // columns, 0), axis=1)


def device_order(shards, replicas, dev_rows):
    width = shards * replicas * dev_rows
    place = jnp.arange(width, dtype=jnp.int32)
    device, rest = place // (shards * dev_rows), place % (shards * dev_rows)
    row = (rest // dev_rows * replicas + device) * dev_rows + rest % dev_rows
    return (place[:, None] == row[None, :]).astype(jnp.bfloat16)


def body(grad, block_owner, left, right, left_root, right_root, moment):
    replicas = lax.axis_size("dp")
    owners = lax.axis_size("fsdp")
    dev_rows, columns_all = grad.shape[2:]
    _, slots, shards, _, _, width = left.shape
    rows = shards * dev_rows
    columns = columns_all // width
    groups = [list(range(i, i + slots)) for i in range(0, replicas, slots)]
    turns = exchange_order(owners)
    pieces = (owners, dev_rows, width)
    by_piece = (slots, shards, dev_rows, width)

    outgoing = call(
        functools.partial(send_rows_kernel, shards),
        jax.ShapeDtypeStruct(pieces, jnp.bfloat16),
        [SMEM, VMEM],
        VMEM,
    )(block_owner, grad.reshape(dev_rows, columns_all))
    arrived = lax.all_to_all(outgoing, "fsdp", split_axis=0, concat_axis=0, tiled=True, axis_index_groups=turns)

    bands = owned_bands(block_owner, lax.axis_index("fsdp"), slots, columns)
    order = device_order(shards, replicas, dev_rows)
    both = jax.ShapeDtypeStruct((2 * rows, width), jnp.bfloat16)
    own_part, *parts = call(
        split_roots_kernel,
        (both,) * slots,
        [VMEM, VMEM, VMEM],
        (VMEM,) * slots,
        [pltpu.VMEM((slots, rows, width), jnp.bfloat16)],
    )(left_root.reshape(slots, rows, width), right_root.reshape(slots, rows, width), order)
    lines = replicas // slots
    devices = [(line, place) for line in range(lines) for place in range(slots)]

    def along_line(part, step):
        pairs = [(i * slots + j, i * slots + (j + step) % slots) for i, j in devices]
        return lax.ppermute(part, "dp", pairs)

    parts = [along_line(part, step) for step, part in enumerate(parts, 1)]
    line_roots = jnp.concatenate([own_part, *parts])
    roots = [line_roots]
    for step in range(1, lines):
        pairs = [(i * slots + j, (i + step) % lines * slots + j) for i, j in devices]
        roots.append(lax.ppermute(line_roots, "dp", pairs))

    early = roots[:2] + roots[3:]
    packed, moment_new = call(
        own_rows_kernel,
        (
            jax.ShapeDtypeStruct((replicas, rows + NORM_ROWS, width), jnp.bfloat16),
            jax.ShapeDtypeStruct(by_piece, jnp.float32),
        ),
        [SMEM, VMEM, VMEM] + [ANY] * len(early),
        (VMEM, VMEM),
        [pltpu.VMEM((rows, width), jnp.float32)],
    )(bands, arrived, moment.reshape(by_piece), *early)
    gathered = lax.all_to_all(packed, "dp", split_axis=0, concat_axis=0, tiled=True)

    results = call(
        functools.partial(block_kernel, rows, slots),
        jax.ShapeDtypeStruct((slots, rows, width), jnp.bfloat16),
        [VMEM] * (2 + lines),
        VMEM,
        [
            pltpu.VMEM((width, width), jnp.float32),
            pltpu.VMEM((width, width), jnp.bfloat16),
            pltpu.VMEM((width, width), jnp.bfloat16),
        ],
    )(gathered, order, *roots)
    back = lax.all_to_all(
        results, "dp", split_axis=0, concat_axis=0, tiled=True, axis_index_groups=groups
    )

    returning = call(
        functools.partial(return_rows_kernel, shards, dev_rows),
        jax.ShapeDtypeStruct(pieces, jnp.bfloat16),
        [SMEM, VMEM],
        VMEM,
    )(bands, back)
    returned = lax.all_to_all(returning, "fsdp", split_axis=0, concat_axis=0, tiled=True, axis_index_groups=turns)

    own_grams, *grams = call(
        functools.partial(gram_kernel, rows),
        (both,) * slots,
        [VMEM, VMEM, ANY],
        (VMEM,) * slots,
        [pltpu.VMEM((width, width), jnp.bfloat16)],
    )(gathered, order, returning)
    grams = [own_grams, *(along_line(part, step) for step, part in enumerate(grams, 1))]
    left_new, right_new = call(
        factors_kernel,
        (jax.ShapeDtypeStruct(by_piece, jnp.float32),) * 2,
        [VMEM] * (2 + slots),
        (VMEM, VMEM),
    )(left.reshape(by_piece), right.reshape(by_piece), *grams)

    update = call(
        functools.partial(place_rows_kernel, shards),
        jax.ShapeDtypeStruct((dev_rows, columns_all), jnp.bfloat16),
        [SMEM, VMEM],
        VMEM,
    )(block_owner, returned)
    return (
        update.reshape(grad.shape),
        left_new.reshape(left.shape),
        right_new.reshape(right.shape),
        moment_new.reshape(moment.shape),
    )


def solution(mesh):
    state = P("fsdp", None, None, "dp", None, None)
    rows = P("fsdp", "dp", None, None)
    return jax.shard_map(
        body,
        mesh=mesh,
        in_specs=(rows, P(), state, state, state, state, state),
        out_specs=(rows, state, state, state),
        check_vma=False,
    )
```

```python
import functools
import jax
import jax.numpy as jnp
from jax import lax
from jax.experimental import pallas as pl
from jax.experimental.pallas import tpu as pltpu
from jax.sharding import PartitionSpec as P

FACTOR_DECAY = 0.999
MOMENT_DECAY = 0.95
ADAM_EPS = 1e-08
NORM_EPS = 1e-06
VMEM_LIMIT = 32 * 1024 * 1024
NORM_ROWS = 8

SMEM = pl.BlockSpec(memory_space=pltpu.SMEM)
VMEM = pl.BlockSpec(memory_space=pltpu.VMEM)
ANY = pl.BlockSpec(memory_space=pl.ANY)


ORDER_STEP = 31
FIRST_OUT = 22
FIRST_BACK = 14


def place_of(owner, owners, first):
    half = owners // 2
    back = pow(ORDER_STEP, -1, half)
    return lax.rem(owner, 2) * half + lax.rem((owner // 2 + half - first) * back, half)


def exchange_order(owners, first):
    half = owners // 2
    chips = [(first + i * ORDER_STEP) % half for i in range(half)]
    return [[2 * chip + core for core in range(2) for chip in chips]]


def call(kernel, out_shape, in_specs, out_specs, scratch_shapes=()):
    return pl.pallas_call(
        kernel,
        out_shape=out_shape,
        in_specs=in_specs,
        out_specs=out_specs,
        scratch_shapes=scratch_shapes,
        compiler_params=pltpu.CompilerParams(vmem_limit_bytes=VMEM_LIMIT),
    )


def exchange(array, axis, groups=None):
    return lax.all_to_all(
        array, axis, split_axis=0, concat_axis=0, tiled=True, axis_index_groups=groups
    )


def dot(a, b, contract=(1, 0)):
    return lax.dot_general(
        a, b, (((contract[0],), (contract[1],)), ((), ())), preferred_element_type=jnp.float32
    )


def send_rows_kernel(shards, owner_ref, grad_ref, out_ref):
    width = out_ref.shape[2]
    count = grad_ref.shape[1] // width
    band = lax.axis_index("fsdp") // shards
    for column in range(count):
        owner = owner_ref[band * count + column]
        out_ref[place_of(owner, out_ref.shape[0], FIRST_OUT)] = grad_ref[:, column * width : (column + 1) * width]


def own_rows_kernel(band_ref, arrived_ref, moment_ref, *refs):
    out_ref, moment_out_ref, rows_ref = refs[-3:]
    slots, shards, dev_rows, width = moment_ref.shape
    owners = arrived_ref.shape[0]
    rows = shards * dev_rows
    copies = out_ref.shape[0] // slots
    for slot in range(slots):
        band = band_ref[slot]
        total = jnp.zeros((dev_rows, width), jnp.float32)
        for shard in range(shards):
            values = arrived_ref[place_of(band * shards + shard, owners, FIRST_OUT)].astype(jnp.float32)
            moment = (
                MOMENT_DECAY * moment_ref[slot, shard] + (1.0 - MOMENT_DECAY) * values * values
            )
            moment_out_ref[slot, shard] = moment
            adam = values / (jnp.sqrt(moment) + ADAM_EPS)
            total += adam * adam
            rows_ref[shard * dev_rows : (shard + 1) * dev_rows, :] = values
        own = rows_ref[...].astype(jnp.bfloat16)
        whole = jnp.sum(total, axis=(0, 1), keepdims=True)
        high = whole.astype(jnp.bfloat16).astype(jnp.float32)
        lane = lax.broadcasted_iota(jnp.int32, (NORM_ROWS, width), 1)
        norm = jnp.where(lane < width // 2, high, whole - high).astype(jnp.bfloat16)
        for copy in range(copies):
            place = copy * slots + slot
            out_ref[place, :rows, :] = own
            out_ref[place, rows:, :] = norm


def split_roots_kernel(left_ref, right_ref, order_ref, *refs):
    out_refs, rows_ref = refs[:-1], refs[-1]
    slots, rows, width = right_ref.shape
    place = lax.rem(lax.axis_index("dp"), slots)
    left = dot(left_ref[...].reshape(slots * rows, width), order_ref[...])
    rows_ref[...] = left.astype(jnp.bfloat16).reshape(slots, rows, width)
    for step, out_ref in enumerate(out_refs):
        slot = lax.rem(place + step, slots)
        out_ref[:rows, :] = rows_ref[slot]
        out_ref[rows:, :] = right_ref[slot]


def block_kernel(rows, slots, arrived_ref, order_ref, *refs):
    *root_refs, out_ref, precond_ref, left_ref, right_ref = refs
    width = order_ref.shape[0]
    span = slots * rows
    device = lax.axis_index("dp")
    first = pl.multiple_of(device // slots * span, span)
    lines = len(root_refs)
    for step, root_ref in enumerate(root_refs):
        line = lax.rem(device // slots + lines - step, lines)
        for part in range(slots):
            source = line * slots + lax.rem(device + slots - part, slots)
            place = pl.ds(pl.multiple_of(source * rows, rows), rows)
            left_ref[place, :] = root_ref[2 * part * rows : (2 * part + 1) * rows, :]
            right_ref[place, :] = root_ref[(2 * part + 1) * rows : (2 * part + 2) * rows, :]
    order = order_ref[...]
    grad = arrived_ref[:, :rows, :].reshape(width, width)
    by_device = dot(grad, order).astype(jnp.bfloat16)
    mixed = dot(left_ref[...], by_device).astype(jnp.bfloat16)
    precond = dot(mixed, right_ref[...])
    precond_ref[...] = precond
    norms = jnp.sum(arrived_ref[:, rows:, :].astype(jnp.float32), axis=0)
    half = width // 2
    adam_total = norms[:1, :1] + norms[:1, half : half + 1]
    precond_total = jnp.sum(precond * precond, axis=(0, 1), keepdims=True)
    scale = jnp.sqrt(adam_total) / jnp.sqrt(precond_total + NORM_EPS)
    update = (precond_ref[pl.ds(first, span), :] * scale).astype(jnp.bfloat16)
    for place in range(slots):
        out_ref[place] = update[place * rows : (place + 1) * rows]


def gram_kernel(rows, arrived_ref, order_ref, _, *refs):
    out_refs, grad_ref = refs[:-1], refs[-1]
    slots = len(out_refs)
    width = order_ref.shape[0]
    device = lax.axis_index("dp")
    order = order_ref[...]
    grad = arrived_ref[:, :rows, :].reshape(width, width)
    by_device = dot(grad, order).astype(jnp.bfloat16)
    grad_ref[...] = by_device
    span = slots * rows
    first = pl.multiple_of(device // slots * span, span)
    left_gram = dot(grad_ref[pl.ds(first, span), :], by_device, (1, 1)).astype(jnp.bfloat16)
    left_gram = dot(left_gram, order, (1, 1)).astype(jnp.bfloat16)
    right_gram = dot(grad_ref[:, pl.ds(first, span)], grad, (0, 0)).astype(jnp.bfloat16)
    for step, out_ref in enumerate(out_refs):
        for place in range(slots):

            @pl.when(lax.rem(device + step, slots) == place)
            def _():
                part = slice(place * rows, (place + 1) * rows)
                out_ref[:rows, :] = left_gram[part]
                out_ref[rows:, :] = right_gram[part]


def return_rows_kernel(shards, dev_rows, band_ref, back_ref, out_ref):
    for slot in range(back_ref.shape[0]):
        band = band_ref[slot]
        for shard in range(shards):
            out_ref[place_of(band * shards + shard, out_ref.shape[0], FIRST_BACK)] = back_ref[
                slot, shard * dev_rows : (shard + 1) * dev_rows, :
            ]


def place_rows_kernel(shards, owner_ref, returned_ref, out_ref):
    width = returned_ref.shape[2]
    count = out_ref.shape[1] // width
    band = lax.axis_index("fsdp") // shards
    for column in range(count):
        owner = owner_ref[band * count + column]
        out_ref[:, column * width : (column + 1) * width] = returned_ref[
            place_of(owner, returned_ref.shape[0], FIRST_BACK)
        ]


def factors_kernel(left_ref, right_ref, *refs):
    gram_refs, out_refs = refs[:-2], refs[-2:]
    slots, shards, dev_rows, _ = left_ref.shape
    rows = shards * dev_rows
    place = lax.rem(lax.axis_index("dp"), slots)
    for step, gram_ref in enumerate(gram_refs):
        slot = lax.rem(place + slots - step, slots)
        for side, (old_ref, out_ref) in enumerate(zip((left_ref, right_ref), out_refs)):
            for shard in range(shards):
                first = side * rows + shard * dev_rows
                gram = gram_ref[first : first + dev_rows, :].astype(jnp.float32)
                out_ref[slot, shard] = (
                    FACTOR_DECAY * old_ref[slot, shard] + (1.0 - FACTOR_DECAY) * gram
                )


def owned_bands(block_owner, owner, slots, columns):
    ids = jnp.arange(block_owner.shape[0], dtype=jnp.int32)
    mine = block_owner == owner
    rank = jnp.sum((mine[None, :] & (ids[None, :] < ids[:, None])).astype(jnp.int32), axis=1)
    slot = jnp.arange(slots, dtype=jnp.int32)
    held = mine[None, :] & (rank[None, :] == slot[:, None])
    return jnp.sum(jnp.where(held, ids[None, :] // columns, 0), axis=1)


def device_order(shards, replicas, dev_rows):
    width = shards * replicas * dev_rows
    place = jnp.arange(width, dtype=jnp.int32)
    device, rest = place // (shards * dev_rows), place % (shards * dev_rows)
    row = (rest // dev_rows * replicas + device) * dev_rows + rest % dev_rows
    return (place[:, None] == row[None, :]).astype(jnp.bfloat16)


def body(grad, block_owner, left, right, left_root, right_root, moment):
    replicas = lax.axis_size("dp")
    owners = lax.axis_size("fsdp")
    dev_rows, columns_all = grad.shape[2:]
    _, slots, shards, _, _, width = left.shape
    rows = shards * dev_rows
    columns = columns_all // width
    groups = [list(range(i, i + slots)) for i in range(0, replicas, slots)]
    out_turns = exchange_order(owners, FIRST_OUT)
    back_turns = exchange_order(owners, FIRST_BACK)
    pieces = (owners, dev_rows, width)
    by_piece = (slots, shards, dev_rows, width)

    outgoing = call(
        functools.partial(send_rows_kernel, shards),
        jax.ShapeDtypeStruct(pieces, jnp.bfloat16),
        [SMEM, VMEM],
        VMEM,
    )(block_owner, grad.reshape(dev_rows, columns_all))
    arrived = exchange(outgoing, "fsdp", out_turns)

    bands = owned_bands(block_owner, lax.axis_index("fsdp"), slots, columns)
    order = device_order(shards, replicas, dev_rows)
    both = jax.ShapeDtypeStruct((2 * rows, width), jnp.bfloat16)
    own_part, *parts = call(
        split_roots_kernel,
        (both,) * slots,
        [VMEM, VMEM, VMEM],
        (VMEM,) * slots,
        [pltpu.VMEM((slots, rows, width), jnp.bfloat16)],
    )(left_root.reshape(slots, rows, width), right_root.reshape(slots, rows, width), order)
    lines = replicas // slots
    devices = [(line, place) for line in range(lines) for place in range(slots)]

    def along_line(part, step):
        pairs = [(i * slots + j, i * slots + (j + step) % slots) for i, j in devices]
        return lax.ppermute(part, "dp", pairs)

    parts = [along_line(part, step) for step, part in enumerate(parts, 1)]
    line_roots = jnp.concatenate([own_part, *parts])
    roots = [line_roots]
    for step in range(1, lines):
        pairs = [(i * slots + j, (i + step) % lines * slots + j) for i, j in devices]
        roots.append(lax.ppermute(line_roots, "dp", pairs))

    packed, moment_new = call(
        own_rows_kernel,
        (
            jax.ShapeDtypeStruct((replicas, rows + NORM_ROWS, width), jnp.bfloat16),
            jax.ShapeDtypeStruct(by_piece, jnp.float32),
        ),
        [SMEM, VMEM, VMEM] + [ANY] * len(roots),
        (VMEM, VMEM),
        [pltpu.VMEM((rows, width), jnp.float32)],
    )(bands, arrived, moment.reshape(by_piece), *roots)
    gathered = lax.all_to_all(packed, "dp", split_axis=0, concat_axis=0, tiled=True)

    results = call(
        functools.partial(block_kernel, rows, slots),
        jax.ShapeDtypeStruct((slots, rows, width), jnp.bfloat16),
        [VMEM] * (2 + lines),
        VMEM,
        [
            pltpu.VMEM((width, width), jnp.float32),
            pltpu.VMEM((width, width), jnp.bfloat16),
            pltpu.VMEM((width, width), jnp.bfloat16),
        ],
    )(gathered, order, *roots)
    back = lax.all_to_all(
        results, "dp", split_axis=0, concat_axis=0, tiled=True, axis_index_groups=groups
    )

    returning = call(
        functools.partial(return_rows_kernel, shards, dev_rows),
        jax.ShapeDtypeStruct(pieces, jnp.bfloat16),
        [SMEM, VMEM],
        VMEM,
    )(bands, back)
    returned = exchange(returning, "fsdp", back_turns)

    own_grams, *grams = call(
        functools.partial(gram_kernel, rows),
        (both,) * slots,
        [VMEM, VMEM, ANY],
        (VMEM,) * slots,
        [pltpu.VMEM((width, width), jnp.bfloat16)],
    )(gathered, order, returning)
    grams = [own_grams, *(along_line(part, step) for step, part in enumerate(grams, 1))]
    left_new, right_new = call(
        factors_kernel,
        (jax.ShapeDtypeStruct(by_piece, jnp.float32),) * 2,
        [VMEM] * (2 + slots),
        (VMEM, VMEM),
    )(left.reshape(by_piece), right.reshape(by_piece), *grams)

    update = call(
        functools.partial(place_rows_kernel, shards),
        jax.ShapeDtypeStruct((dev_rows, columns_all), jnp.bfloat16),
        [SMEM, VMEM],
        VMEM,
    )(block_owner, returned)
    return (
        update.reshape(grad.shape),
        left_new.reshape(left.shape),
        right_new.reshape(right.shape),
        moment_new.reshape(moment.shape),
    )


def solution(mesh):
    state = P("fsdp", None, None, "dp", None, None)
    rows = P("fsdp", "dp", None, None)
    return jax.shard_map(
        body,
        mesh=mesh,
        in_specs=(rows, P(), state, state, state, state, state),
        out_specs=(rows, state, state, state),
        check_vma=False,
    )
```

```python
import functools
import jax
import jax.numpy as jnp
from jax import lax
from jax.experimental import pallas as pl
from jax.experimental.pallas import tpu as pltpu
from jax.sharding import PartitionSpec as P

FACTOR_DECAY = 0.999
MOMENT_DECAY = 0.95
ADAM_EPS = 1e-08
NORM_EPS = 1e-06
VMEM_LIMIT = 32 * 1024 * 1024
NORM_ROWS = 8

SMEM = pl.BlockSpec(memory_space=pltpu.SMEM)
VMEM = pl.BlockSpec(memory_space=pltpu.VMEM)
ANY = pl.BlockSpec(memory_space=pl.ANY)


ORDER_STEP = 31
FIRST_OUT = 24
FIRST_BACK = 16


def place_of(owner, owners, first):
    half = owners // 2
    back = pow(ORDER_STEP, -1, half)
    return (owner & 1) * half + ((((owner >> 1) - first) * back) & (half - 1))


def exchange_order(owners, first):
    half = owners // 2
    chips = [(first + i * ORDER_STEP) % half for i in range(half)]
    return [[2 * chip + core for core in range(2) for chip in chips]]


def call(kernel, out_shape, in_specs, out_specs, scratch_shapes=()):
    return pl.pallas_call(
        kernel,
        out_shape=out_shape,
        in_specs=in_specs,
        out_specs=out_specs,
        scratch_shapes=scratch_shapes,
        compiler_params=pltpu.CompilerParams(vmem_limit_bytes=VMEM_LIMIT),
    )


def exchange(array, axis, groups=None):
    return lax.all_to_all(
        array, axis, split_axis=0, concat_axis=0, tiled=True, axis_index_groups=groups
    )


def dot(a, b, contract=(1, 0)):
    return lax.dot_general(
        a, b, (((contract[0],), (contract[1],)), ((), ())), preferred_element_type=jnp.float32
    )


def send_rows_kernel(shards, owner_ref, grad_ref, out_ref):
    width = out_ref.shape[2]
    count = grad_ref.shape[1] // width
    band = lax.axis_index("fsdp") // shards
    for column in range(count):
        owner = owner_ref[band * count + column]
        out_ref[place_of(owner, out_ref.shape[0], FIRST_OUT)] = grad_ref[:, column * width : (column + 1) * width]


def own_rows_kernel(band_ref, arrived_ref, moment_ref, *refs):
    out_ref, moment_out_ref, rows_ref = refs[-3:]
    slots, shards, dev_rows, width = moment_ref.shape
    owners = arrived_ref.shape[0]
    rows = shards * dev_rows
    copies = out_ref.shape[0] // slots
    for slot in range(slots):
        band = band_ref[slot]
        total = jnp.zeros((dev_rows, width), jnp.float32)
        for shard in range(shards):
            values = arrived_ref[place_of(band * shards + shard, owners, FIRST_OUT)].astype(jnp.float32)
            moment = (
                MOMENT_DECAY * moment_ref[slot, shard] + (1.0 - MOMENT_DECAY) * values * values
            )
            moment_out_ref[slot, shard] = moment
            adam = values / (jnp.sqrt(moment) + ADAM_EPS)
            total += adam * adam
            rows_ref[shard * dev_rows : (shard + 1) * dev_rows, :] = values
        own = rows_ref[...].astype(jnp.bfloat16)
        whole = jnp.sum(total, axis=(0, 1), keepdims=True)
        high = whole.astype(jnp.bfloat16).astype(jnp.float32)
        lane = lax.broadcasted_iota(jnp.int32, (NORM_ROWS, width), 1)
        norm = jnp.where(lane < width // 2, high, whole - high).astype(jnp.bfloat16)
        for copy in range(copies):
            place = copy * slots + slot
            out_ref[place, :rows, :] = own
            out_ref[place, rows:, :] = norm


def split_roots_kernel(left_ref, right_ref, order_ref, *refs):
    out_refs, rows_ref = refs[:-1], refs[-1]
    slots, rows, width = right_ref.shape
    place = lax.rem(lax.axis_index("dp"), slots)
    left = dot(left_ref[...].reshape(slots * rows, width), order_ref[...])
    rows_ref[...] = left.astype(jnp.bfloat16).reshape(slots, rows, width)
    for step, out_ref in enumerate(out_refs):
        slot = lax.rem(place + step, slots)
        out_ref[:rows, :] = rows_ref[slot]
        out_ref[rows:, :] = right_ref[slot]


def block_kernel(rows, slots, arrived_ref, order_ref, *refs):
    *root_refs, out_ref, precond_ref, left_ref, right_ref = refs
    width = order_ref.shape[0]
    span = slots * rows
    device = lax.axis_index("dp")
    first = pl.multiple_of(device // slots * span, span)
    lines = len(root_refs)
    for step, root_ref in enumerate(root_refs):
        line = lax.rem(device // slots + lines - step, lines)
        for part in range(slots):
            source = line * slots + lax.rem(device + slots - part, slots)
            place = pl.ds(pl.multiple_of(source * rows, rows), rows)
            left_ref[place, :] = root_ref[2 * part * rows : (2 * part + 1) * rows, :]
            right_ref[place, :] = root_ref[(2 * part + 1) * rows : (2 * part + 2) * rows, :]
    order = order_ref[...]
    grad = arrived_ref[:, :rows, :].reshape(width, width)
    by_device = dot(grad, order).astype(jnp.bfloat16)
    mixed = dot(left_ref[...], by_device).astype(jnp.bfloat16)
    precond = dot(mixed, right_ref[...])
    precond_ref[...] = precond
    norms = jnp.sum(arrived_ref[:, rows:, :].astype(jnp.float32), axis=0)
    half = width // 2
    adam_total = norms[:1, :1] + norms[:1, half : half + 1]
    precond_total = jnp.sum(precond * precond, axis=(0, 1), keepdims=True)
    scale = jnp.sqrt(adam_total) / jnp.sqrt(precond_total + NORM_EPS)
    update = (precond_ref[pl.ds(first, span), :] * scale).astype(jnp.bfloat16)
    for place in range(slots):
        out_ref[place] = update[place * rows : (place + 1) * rows]


def gram_kernel(rows, arrived_ref, order_ref, _, *refs):
    out_refs, grad_ref = refs[:-1], refs[-1]
    slots = len(out_refs)
    width = order_ref.shape[0]
    device = lax.axis_index("dp")
    order = order_ref[...]
    grad = arrived_ref[:, :rows, :].reshape(width, width)
    by_device = dot(grad, order).astype(jnp.bfloat16)
    grad_ref[...] = by_device
    span = slots * rows
    first = pl.multiple_of(device // slots * span, span)
    left_gram = dot(grad_ref[pl.ds(first, span), :], by_device, (1, 1)).astype(jnp.bfloat16)
    left_gram = dot(left_gram, order, (1, 1)).astype(jnp.bfloat16)
    right_gram = dot(grad_ref[:, pl.ds(first, span)], grad, (0, 0)).astype(jnp.bfloat16)
    for step, out_ref in enumerate(out_refs):
        for place in range(slots):

            @pl.when(lax.rem(device + step, slots) == place)
            def _():
                part = slice(place * rows, (place + 1) * rows)
                out_ref[:rows, :] = left_gram[part]
                out_ref[rows:, :] = right_gram[part]


def return_rows_kernel(shards, dev_rows, band_ref, back_ref, out_ref):
    for slot in range(back_ref.shape[0]):
        band = band_ref[slot]
        for shard in range(shards):
            out_ref[place_of(band * shards + shard, out_ref.shape[0], FIRST_BACK)] = back_ref[
                slot, shard * dev_rows : (shard + 1) * dev_rows, :
            ]


def place_rows_kernel(shards, owner_ref, returned_ref, out_ref):
    width = returned_ref.shape[2]
    count = out_ref.shape[1] // width
    band = lax.axis_index("fsdp") // shards
    for column in range(count):
        owner = owner_ref[band * count + column]
        out_ref[:, column * width : (column + 1) * width] = returned_ref[
            place_of(owner, returned_ref.shape[0], FIRST_BACK)
        ]


def factors_kernel(left_ref, right_ref, *refs):
    gram_refs, out_refs = refs[:-2], refs[-2:]
    slots, shards, dev_rows, _ = left_ref.shape
    rows = shards * dev_rows
    place = lax.rem(lax.axis_index("dp"), slots)
    for step, gram_ref in enumerate(gram_refs):
        slot = lax.rem(place + slots - step, slots)
        for side, (old_ref, out_ref) in enumerate(zip((left_ref, right_ref), out_refs)):
            for shard in range(shards):
                first = side * rows + shard * dev_rows
                gram = gram_ref[first : first + dev_rows, :].astype(jnp.float32)
                out_ref[slot, shard] = (
                    FACTOR_DECAY * old_ref[slot, shard] + (1.0 - FACTOR_DECAY) * gram
                )


def owned_bands(block_owner, owner, slots, columns):
    ids = jnp.arange(block_owner.shape[0], dtype=jnp.int32)
    mine = block_owner == owner
    rank = jnp.sum((mine[None, :] & (ids[None, :] < ids[:, None])).astype(jnp.int32), axis=1)
    slot = jnp.arange(slots, dtype=jnp.int32)
    held = mine[None, :] & (rank[None, :] == slot[:, None])
    return jnp.sum(jnp.where(held, ids[None, :] // columns, 0), axis=1)


def device_order(shards, replicas, dev_rows):
    width = shards * replicas * dev_rows
    place = jnp.arange(width, dtype=jnp.int32)
    device, rest = place // (shards * dev_rows), place % (shards * dev_rows)
    row = (rest // dev_rows * replicas + device) * dev_rows + rest % dev_rows
    return (place[:, None] == row[None, :]).astype(jnp.bfloat16)


def body(grad, block_owner, left, right, left_root, right_root, moment):
    replicas = lax.axis_size("dp")
    owners = lax.axis_size("fsdp")
    dev_rows, columns_all = grad.shape[2:]
    _, slots, shards, _, _, width = left.shape
    rows = shards * dev_rows
    columns = columns_all // width
    groups = [list(range(i, i + slots)) for i in range(0, replicas, slots)]
    out_turns = exchange_order(owners, FIRST_OUT)
    back_turns = exchange_order(owners, FIRST_BACK)
    pieces = (owners, dev_rows, width)
    by_piece = (slots, shards, dev_rows, width)

    outgoing = call(
        functools.partial(send_rows_kernel, shards),
        jax.ShapeDtypeStruct(pieces, jnp.bfloat16),
        [SMEM, VMEM],
        VMEM,
    )(block_owner, grad.reshape(dev_rows, columns_all))
    arrived = exchange(outgoing, "fsdp", out_turns)

    bands = owned_bands(block_owner, lax.axis_index("fsdp"), slots, columns)
    order = device_order(shards, replicas, dev_rows)
    both = jax.ShapeDtypeStruct((2 * rows, width), jnp.bfloat16)
    own_part, *parts = call(
        split_roots_kernel,
        (both,) * slots,
        [VMEM, VMEM, VMEM],
        (VMEM,) * slots,
        [pltpu.VMEM((slots, rows, width), jnp.bfloat16)],
    )(left_root.reshape(slots, rows, width), right_root.reshape(slots, rows, width), order)
    lines = replicas // slots
    devices = [(line, place) for line in range(lines) for place in range(slots)]

    def along_line(part, step):
        pairs = [(i * slots + j, i * slots + (j + step) % slots) for i, j in devices]
        return lax.ppermute(part, "dp", pairs)

    parts = [along_line(part, step) for step, part in enumerate(parts, 1)]
    line_roots = jnp.concatenate([own_part, *parts])
    roots = [line_roots]
    for step in range(1, lines):
        pairs = [(i * slots + j, (i + step) % lines * slots + j) for i, j in devices]
        roots.append(lax.ppermute(line_roots, "dp", pairs))

    packed, moment_new = call(
        own_rows_kernel,
        (
            jax.ShapeDtypeStruct((replicas, rows + NORM_ROWS, width), jnp.bfloat16),
            jax.ShapeDtypeStruct(by_piece, jnp.float32),
        ),
        [SMEM, VMEM, VMEM] + [ANY] * len(roots),
        (VMEM, VMEM),
        [pltpu.VMEM((rows, width), jnp.float32)],
    )(bands, arrived, moment.reshape(by_piece), *roots)
    gathered = lax.all_to_all(packed, "dp", split_axis=0, concat_axis=0, tiled=True)

    results = call(
        functools.partial(block_kernel, rows, slots),
        jax.ShapeDtypeStruct((slots, rows, width), jnp.bfloat16),
        [VMEM] * (2 + lines),
        VMEM,
        [
            pltpu.VMEM((width, width), jnp.float32),
            pltpu.VMEM((width, width), jnp.bfloat16),
            pltpu.VMEM((width, width), jnp.bfloat16),
        ],
    )(gathered, order, *roots)
    back = lax.all_to_all(
        results, "dp", split_axis=0, concat_axis=0, tiled=True, axis_index_groups=groups
    )

    returning = call(
        functools.partial(return_rows_kernel, shards, dev_rows),
        jax.ShapeDtypeStruct(pieces, jnp.bfloat16),
        [SMEM, VMEM],
        VMEM,
    )(bands, back)
    returned = exchange(returning, "fsdp", back_turns)

    own_grams, *grams = call(
        functools.partial(gram_kernel, rows),
        (both,) * slots,
        [VMEM, VMEM, ANY],
        (VMEM,) * slots,
        [pltpu.VMEM((width, width), jnp.bfloat16)],
    )(gathered, order, returning)
    grams = [own_grams, *(along_line(part, step) for step, part in enumerate(grams, 1))]
    left_new, right_new = call(
        factors_kernel,
        (jax.ShapeDtypeStruct(by_piece, jnp.float32),) * 2,
        [VMEM] * (2 + slots),
        (VMEM, VMEM),
    )(left.reshape(by_piece), right.reshape(by_piece), *grams)

    update = call(
        functools.partial(place_rows_kernel, shards),
        jax.ShapeDtypeStruct((dev_rows, columns_all), jnp.bfloat16),
        [SMEM, VMEM],
        VMEM,
    )(block_owner, returned)
    return (
        update.reshape(grad.shape),
        left_new.reshape(left.shape),
        right_new.reshape(right.shape),
        moment_new.reshape(moment.shape),
    )


def solution(mesh):
    state = P("fsdp", None, None, "dp", None, None)
    rows = P("fsdp", "dp", None, None)
    return jax.shard_map(
        body,
        mesh=mesh,
        in_specs=(rows, P(), state, state, state, state, state),
        out_specs=(rows, state, state, state),
        check_vma=False,
    )
```
